32 devices in a mesh: parts: 2 (over x), ep: 16 (over z, y, core).
Axes of the slice: x: 2, y: 2, z: 4, core: 2. Of those that a mesh axis runs over, the one named last changes fastest.
Arguments:
- tokens: bfloat16 [4096, 7168], P(('parts', 'ep')), parts along dimension 0, may hold values from -6 to 6
- cotangent: bfloat16 [4096, 7168], P(('parts', 'ep')), parts along dimension 0, may hold values from -6 to 6
- expert_ids: int32 [4096, 8], P(('parts', 'ep')), parts along dimension 0, may hold values from 0 to 255, as said below
- route_weight: float32 [4096, 8], P(('parts', 'ep')), parts along dimension 0, may hold values from 0.05 to 0.6
- gate_weight: bfloat16 [7168, 2048], P(None, 'ep'), may hold values from -0.0625 to 0.0625
- up_weight: bfloat16 [7168, 2048], P(None, 'ep'), may hold values from -0.0625 to 0.0625
- down_weight: bfloat16 [2048, 7168], P('ep'), may hold values from -0.125 to 0.125
Outputs:
- mixed: bfloat16 [4096, 7168], P(('parts', 'ep')), parts along dimension 0
- grad_tokens: bfloat16 [4096, 7168], P(('parts', 'ep')), parts along dimension 0
- grad_route: float32 [4096, 8], P(('parts', 'ep')), parts along dimension 0
The draws below stay inside these ranges and needn't reach their ends.
There are 2 independent parts, one for each index of `parts`. The reference program is written for one: setup_inputs(seed, part) draws one part's arguments, and reference() takes and returns one part's arrays. A program takes and returns all parts, laid end to end along the dimension named above; an argument that names none is the same for every part. Nothing has to cross between parts.
Inputs may be any that keep to these rules, and one draw needn't show every extreme that they name: `expert_ids`: each row names 8 different experts. Of the experts in flight 0 to 0, each is named by at most 8 of the 128 rows of one device, and one of them is named by exactly 8 rows of every device.
All inputs are finite; a program needn't handle non-finite values.
Results may differ from the reference program's by a relative error of at most 0.0065.
Values may be sent and summed in bfloat16 or wider, within the bound.
No kernel may reach another device: no remote copies, remote signals or barrier semaphores. Data moves between devices by JAX's collectives and lax.ppermute only.
A program may use at most 128 MiB of HBM per device.

```python
import jax
import jax.numpy as jnp
from jax import lax

D = 7168
FF = 2048
EXPERTS = 256
TOP = 8
GROUP = 16
SLOT = 8
TOK_DEV = 128
H_DEV = 128
E_WIN = 1
TOKENS = 2048
N_EP = 16


def draw_expert_ids(key, part):
    key = jax.random.fold_in(key, 7)
    keys = jax.random.split(key, 5)
    hottest = jax.random.randint(keys[0], (), 0, E_WIN, dtype=jnp.int32)
    counts = jax.random.randint(keys[1], (N_EP, E_WIN), 1, SLOT + 1, dtype=jnp.int32)
    window = jnp.arange(E_WIN, dtype=jnp.int32)
    counts = jnp.where(window[None, :] == hottest, SLOT, counts)
    token_index = jnp.arange(TOK_DEV, dtype=jnp.int32)
    scores = jax.random.randint(keys[2], (N_EP, E_WIN, TOK_DEV), 0, 65536, dtype=jnp.int32) * TOK_DEV + token_index[None, None, :]
    ranks = jnp.argsort(jnp.argsort(scores, axis=2), axis=2).astype(jnp.int32)
    chosen = ranks < counts[:, :, None]
    chosen = jnp.transpose(chosen, (0, 2, 1)).reshape(TOKENS, E_WIN)
    rest = EXPERTS - E_WIN
    fill_scores = jax.random.randint(keys[3], (TOKENS, rest), 0, 65536, dtype=jnp.int32) * 256 + jnp.arange(rest, dtype=jnp.int32)[None, :]
    filler = jnp.argsort(fill_scores, axis=1)[:, :TOP].astype(jnp.int32) + E_WIN
    taken = jnp.sum(chosen.astype(jnp.int32), axis=1)
    order = jnp.cumsum(chosen.astype(jnp.int32), axis=1) - 1
    slot_index = jnp.arange(TOP, dtype=jnp.int32)
    match = chosen[:, None, :] & (order[:, None, :] == slot_index[None, :, None])
    window_pick = jnp.sum(jnp.where(match, window[None, None, :], 0), axis=2).astype(jnp.int32)
    fill_index = jnp.maximum(slot_index[None, :] - taken[:, None], 0).astype(jnp.int32)
    fill_pick = jnp.take_along_axis(filler, fill_index, axis=1)
    ids = jnp.where(slot_index[None, :] < taken[:, None], window_pick, fill_pick)
    shuffle_scores = jax.random.randint(keys[4], (TOKENS, TOP), 0, 65536, dtype=jnp.int32) * TOP + slot_index[None, :]
    shuffle = jnp.argsort(shuffle_scores, axis=1).astype(jnp.int32)
    return jnp.take_along_axis(ids, shuffle, axis=1).astype(jnp.int32)


def block_scale(stream_key, extent, cuts, low, high):
    def one(position, parts):
        steps = jax.random.uniform(jax.random.fold_in(jax.random.fold_in(stream_key, 6), position), (parts,), jnp.float32, low / len(cuts), high / len(cuts))
        return jnp.repeat(jnp.exp(steps), extent[position] // parts).reshape((-1,) + (1,) * (len(extent) - position - 1))

    gain = one(*cuts[0])
    for cut in cuts[1:]:
        gain = gain * one(*cut)
    return gain


def scatter_about(stream_key, dims, deviation, reach, pieces=(), kind=jnp.bfloat16):
    values = jax.random.normal(stream_key, dims, jnp.float32) * deviation
    if len(pieces) > 0:
        values = block_scale(stream_key, dims, pieces, -0.22, 0.18) * values
    return jnp.clip(values, min=-reach, max=reach).astype(kind)


def setup_inputs(seed: int = 0, part: int = 0) -> dict:
    streams_of = jax.random.split(jax.random.key(seed), 8)
    own_keys = jax.random.split(jax.random.fold_in(streams_of[7], part), 8)
    tokens = scatter_about(own_keys[0], (TOKENS, D), 1.0, 6.0, ((0, 16),))
    cotangent = scatter_about(own_keys[1], (TOKENS, D), 1.0, 6.0, ((0, 16),))
    expert_ids = draw_expert_ids(jax.random.fold_in(jax.random.fold_in(streams_of[7], part), 71), part)
    route_weight = jnp.clip(0.05 + 0.55 * jax.random.uniform(own_keys[3], (TOKENS, TOP), jnp.float32) ** block_scale(own_keys[3], (TOKENS, TOP), ((0, 16),), -0.2, 0.2), 0.05, 0.6)
    gate_weight = scatter_about(streams_of[4], (D, E_WIN * FF), D ** -0.5, 0.0625, ((1, 16),))
    up_weight = scatter_about(streams_of[5], (D, E_WIN * FF), D ** -0.5, 0.0625, ((1, 16),))
    down_weight = scatter_about(streams_of[6], (E_WIN * FF, D), FF ** -0.5, 0.125, ((0, 16),))
    return dict(tokens=tokens, cotangent=cotangent, expert_ids=expert_ids, route_weight=route_weight, gate_weight=gate_weight, up_weight=up_weight, down_weight=down_weight)


def silu_parts(pre):
    sigmoid_val = jax.nn.sigmoid(pre)
    return pre * sigmoid_val, sigmoid_val


def group_sum(terms):
    rounded = lax.optimization_barrier(terms.astype(jnp.bfloat16))
    return jnp.sum(rounded.astype(jnp.float32), axis=0)


def reference(tokens, cotangent, expert_ids, route_weight, gate_weight, up_weight, down_weight):
    window = jnp.arange(E_WIN, dtype=jnp.int32)
    onehot = expert_ids[:, :, None] == window[None, None, :]
    chosen = jnp.any(onehot, axis=1)
    counted = chosen.astype(jnp.int32).reshape(N_EP, TOK_DEV, E_WIN)
    places = (jnp.cumsum(counted, axis=1) - 1).reshape(TOKENS, E_WIN).astype(jnp.int32)
    blocks = (jnp.arange(TOKENS, dtype=jnp.int32) // TOK_DEV)[:, None]
    capacity = N_EP * SLOT
    slot_rows = jnp.where(chosen, blocks * SLOT + places, capacity).astype(jnp.int32)
    weight_sel = jnp.sum(jnp.where(onehot, route_weight[:, :, None], 0.0), axis=1)
    cot_wide = cotangent.astype(jnp.float32)
    mixed = jnp.zeros((TOKENS, D), jnp.float32)
    grad_sum = jnp.zeros((TOKENS, D), jnp.float32)
    route_dots = []
    for expert in range(E_WIN):
        target = slot_rows[:, expert]
        live = chosen[:, expert:expert + 1]
        rows_in = jnp.zeros((capacity, D), jnp.bfloat16).at[target].set(tokens, mode="drop")
        scaled = (weight_sel[:, expert:expert + 1] * cot_wide).astype(jnp.bfloat16)
        rows_grad = jnp.zeros((capacity, D), jnp.bfloat16).at[target].set(scaled, mode="drop")
        gate_cols = gate_weight[:, expert * FF:(expert + 1) * FF]
        up_cols = up_weight[:, expert * FF:(expert + 1) * FF]
        down_rows = down_weight[expert * FF:(expert + 1) * FF]
        gate_act = jnp.dot(rows_in, gate_cols, preferred_element_type=jnp.float32)
        up_act = jnp.dot(rows_in, up_cols, preferred_element_type=jnp.float32)
        silu_val, sigmoid_val = silu_parts(gate_act)
        hidden_act = (silu_val * up_act).astype(jnp.bfloat16)
        split_hidden = hidden_act.astype(jnp.float32).reshape(capacity, GROUP, H_DEV)
        split_down = down_rows.astype(jnp.float32).reshape(GROUP, H_DEV, D)
        expert_out = group_sum(jnp.einsum("rgh,ghd->grd", split_hidden, split_down))
        back_hidden = jnp.dot(rows_grad, down_rows.T, preferred_element_type=jnp.float32)
        grad_gate = (back_hidden * up_act * sigmoid_val * (1.0 + gate_act * (1.0 - sigmoid_val))).astype(jnp.bfloat16)
        grad_up = (back_hidden * silu_val).astype(jnp.bfloat16)
        split_gg = grad_gate.astype(jnp.float32).reshape(capacity, GROUP, H_DEV)
        split_gu = grad_up.astype(jnp.float32).reshape(capacity, GROUP, H_DEV)
        split_gate = gate_cols.astype(jnp.float32).reshape(D, GROUP, H_DEV)
        split_up = up_cols.astype(jnp.float32).reshape(D, GROUP, H_DEV)
        input_terms = jnp.einsum("rgh,dgh->grd", split_gg, split_gate) + jnp.einsum("rgh,dgh->grd", split_gu, split_up)
        input_term = group_sum(input_terms)
        safe_rows = jnp.minimum(target, capacity - 1).astype(jnp.int32)
        picked_out = expert_out[safe_rows]
        picked_in = input_term[safe_rows]
        mixed = mixed + jnp.where(live, weight_sel[:, expert:expert + 1] * picked_out, 0.0)
        grad_sum = grad_sum + jnp.where(live, picked_in, 0.0)
        route_dots.append(jnp.where(chosen[:, expert], jnp.sum(cot_wide * picked_out, axis=1), 0.0))
    dots = jnp.stack(route_dots, axis=1)
    grad_route = jnp.sum(jnp.where(onehot, dots[:, None, :], 0.0), axis=2)
    return mixed.astype(jnp.bfloat16), grad_sum.astype(jnp.bfloat16), grad_route
```

```python
import jax
import jax.numpy as jnp
from jax import lax
from jax.sharding import PartitionSpec as P

GROUP = 16
SLOT = 8
RING = (0, 2, 4, 6, 7, 5, 3, 1)


def expert_terms(received, gate_weight, up_weight, down_weight):
    sources = received.shape[0]
    slot_count = received.shape[2]
    width_model = received.shape[3]
    in_rows = received[:, 0].reshape(sources * slot_count, width_model)
    grad_rows = received[:, 1].reshape(sources * slot_count, width_model)
    gate_act = jnp.dot(in_rows, gate_weight, preferred_element_type=jnp.float32)
    up_act = jnp.dot(in_rows, up_weight, preferred_element_type=jnp.float32)
    sigmoid_val = jax.nn.sigmoid(gate_act)
    silu_val = gate_act * sigmoid_val
    hidden_act = (silu_val * up_act).astype(jnp.bfloat16)
    out_part = jnp.dot(hidden_act, down_weight, preferred_element_type=jnp.float32).astype(
        jnp.bfloat16
    )
    back_hidden = jnp.dot(grad_rows, down_weight.T, preferred_element_type=jnp.float32)
    grad_gate = (
        back_hidden * up_act * sigmoid_val * (1.0 + gate_act * (1.0 - sigmoid_val))
    ).astype(jnp.bfloat16)
    grad_up = (back_hidden * silu_val).astype(jnp.bfloat16)
    input_part = (
        jnp.dot(grad_gate, gate_weight.T, preferred_element_type=jnp.float32)
        + jnp.dot(grad_up, up_weight.T, preferred_element_type=jnp.float32)
    ).astype(jnp.bfloat16)
    return out_part, input_part


def pick_rows(tokens, cotangent, expert_ids, route_weight, experts_win):
    window = jnp.arange(experts_win, dtype=jnp.int32)
    onehot = expert_ids[:, :, None] == window[None, None, :]
    chosen = jnp.any(onehot, axis=1)
    places = jnp.cumsum(chosen.astype(jnp.int32), axis=0) - 1
    weight_sel = jnp.sum(jnp.where(onehot, route_weight[:, :, None], 0.0), axis=1)
    slot_index = jnp.arange(SLOT, dtype=jnp.int32)
    picker_mask = chosen.T[:, None, :] & (places.T[:, None, :] == slot_index[None, :, None])
    picker = picker_mask.astype(jnp.bfloat16)
    picker_wide = picker_mask.astype(jnp.float32)
    rows_x = jnp.einsum("est,td->esd", picker, tokens, preferred_element_type=jnp.float32).astype(
        jnp.bfloat16
    )
    rows_cot = jnp.einsum(
        "est,td->esd", picker, cotangent, preferred_element_type=jnp.float32
    ).astype(jnp.bfloat16)
    slot_weight = jnp.sum(picker_wide * weight_sel.T[:, None, :], axis=2)
    rows_dy = (rows_cot.astype(jnp.float32) * slot_weight[:, :, None]).astype(jnp.bfloat16)
    return onehot, picker_wide, weight_sel, rows_x, rows_cot, rows_dy


def any_size(tokens, cotangent, expert_ids, route_weight, gate_weight, up_weight, down_weight):
    width_model = tokens.shape[1]
    devices = lax.axis_size("ep")
    experts_win = devices // GROUP
    onehot, picker_wide, weight_sel, rows_x, rows_cot, rows_dy = pick_rows(
        tokens, cotangent, expert_ids, route_weight, experts_win
    )
    packed = jnp.stack([rows_x, rows_dy], axis=1)
    outgoing = jnp.repeat(packed, GROUP, axis=0)
    out_part, input_part = expert_terms(
        lax.all_to_all(outgoing, "ep", split_axis=0, concat_axis=0, tiled=True),
        gate_weight,
        up_weight,
        down_weight,
    )
    shape = (devices, SLOT, width_model)
    terms = jnp.stack([out_part.reshape(shape), input_part.reshape(shape)], axis=1)
    back = lax.all_to_all(terms, "ep", split_axis=0, concat_axis=0, tiled=True)
    summed = jnp.sum(
        back.reshape(experts_win, GROUP, 2, SLOT, width_model), axis=1, dtype=jnp.float32
    )
    expert_out = summed[:, 0]
    input_term = summed[:, 1]
    weighted_picker = picker_wide * weight_sel.T[:, None, :]
    mixed = jnp.einsum("est,esd->td", weighted_picker, expert_out, precision=lax.Precision.HIGHEST)
    grad_tokens = jnp.einsum(
        "est,esd->td", picker_wide, input_term, precision=lax.Precision.HIGHEST
    )
    slot_dots = jnp.sum(rows_cot.astype(jnp.float32) * expert_out, axis=2)
    token_dots = jnp.einsum("est,es->te", picker_wide, slot_dots, precision=lax.Precision.HIGHEST)
    grad_route = jnp.sum(jnp.where(onehot, token_dots[:, None, :], 0.0), axis=2)
    return (mixed.astype(jnp.bfloat16), grad_tokens.astype(jnp.bfloat16), grad_route)


def hop(step):
    pairs = []
    for place, chip in enumerate(RING):
        target = RING[(place + step) % len(RING)]
        pairs += [(2 * chip, 2 * target), (2 * chip + 1, 2 * target + 1)]
    return pairs


NEXT = hop(1)
PREV = hop(-1)
SWAP = [(i, i ^ 1) for i in range(GROUP)]


def send(value, pairs):
    return lax.ppermute(value, "ep", pairs)


def ring_gather(own):
    half = own.shape[1] // 2
    right = left = own
    mine = [own]
    other = [send(own, SWAP)]
    for _ in range(3):
        right, left = send(right, NEXT), send(left, PREV)
        mine += [right, left]
        other += [send(right, SWAP), send(left, SWAP)]
    right, left = send(right[:, :half], NEXT), send(left[:, half:], PREV)
    mine.append(jnp.concatenate([right, left], axis=1))
    other.append(jnp.concatenate([send(right, SWAP), send(left, SWAP)], axis=1))
    return mine, other


def ring_sum(part):
    width = part.shape[1]
    half = width // 2
    pieces = part.reshape(8, 2, SLOT, width)

    def chip(j):
        return pieces[j, 0].astype(jnp.float32) + send(pieces[j, 1], SWAP).astype(jnp.float32)

    far = chip(7).astype(jnp.bfloat16)
    right, left = send(far[:, :half], NEXT), send(far[:, half:], PREV)
    up, down = chip(6), chip(5)
    right = jnp.concatenate([up[:, :half] + right.astype(jnp.float32), up[:, half:]], axis=1)
    left = jnp.concatenate([down[:, :half], down[:, half:] + left.astype(jnp.float32)], axis=1)
    right, left = send(right.astype(jnp.bfloat16), NEXT), send(left.astype(jnp.bfloat16), PREV)
    for j in (4, 2):
        right = (chip(j) + right.astype(jnp.float32)).astype(jnp.bfloat16)
        left = (chip(j - 1) + left.astype(jnp.float32)).astype(jnp.bfloat16)
        right, left = send(right, NEXT), send(left, PREV)
    return chip(0) + right.astype(jnp.float32) + left.astype(jnp.float32)


def one_group(tokens, cotangent, expert_ids, route_weight, gate_weight, up_weight, down_weight):
    onehot, picker_wide, weight_sel, rows_x, rows_cot, rows_dy = pick_rows(
        tokens, cotangent, expert_ids, route_weight, 1
    )
    mine_x, other_x = ring_gather(rows_x[0])
    mine_dy, other_dy = ring_gather(rows_dy[0])
    all_x = jnp.stack([v for pair in zip(mine_x, other_x) for v in pair])
    all_dy = jnp.stack([v for pair in zip(mine_dy, other_dy) for v in pair])
    out_part, input_part = expert_terms(
        jnp.stack([all_x, all_dy], axis=1), gate_weight, up_weight, down_weight
    )
    expert_out = ring_sum(out_part)
    input_term = ring_sum(input_part)
    slot_weight = jnp.sum(picker_wide[0] * weight_sel.T, axis=1)
    picker = picker_wide[0].astype(jnp.bfloat16)
    weighted = (expert_out * slot_weight[:, None]).astype(jnp.bfloat16)
    mixed = jnp.einsum("st,sd->td", picker, weighted, preferred_element_type=jnp.float32)
    grad_tokens = jnp.einsum(
        "st,sd->td", picker, input_term.astype(jnp.bfloat16), preferred_element_type=jnp.float32
    )
    slot_dots = jnp.sum(rows_cot[0].astype(jnp.float32) * expert_out, axis=1)
    token_dots = jnp.sum(picker_wide[0] * slot_dots[:, None], axis=0)
    grad_route = jnp.where(onehot[:, :, 0], token_dots[:, None], 0.0)
    return (mixed.astype(jnp.bfloat16), grad_tokens.astype(jnp.bfloat16), grad_route)


def body(*args):
    if lax.axis_size("ep") == GROUP:
        return one_group(*args)
    return any_size(*args)


def solution(mesh):
    return jax.shard_map(
        body,
        mesh=mesh,
        in_specs=(
            P(("parts", "ep"), None),
            P(("parts", "ep"), None),
            P(("parts", "ep"), None),
            P(("parts", "ep"), None),
            P(None, "ep"),
            P(None, "ep"),
            P("ep", None),
        ),
        out_specs=(P(("parts", "ep"), None), P(("parts", "ep"), None), P(("parts", "ep"), None)),
        check_vma=False,
    )
```
